32 devices in a mesh: groups: 2 (over y), seq: 4 (over z), head: 4 (over x, core).
Axes of the slice: x: 2, y: 2, z: 4, core: 2. Of those that a mesh axis runs over, the one named last changes fastest.
Arguments:
- raw_tokens: bfloat16 [4096, 4096], P(('groups', 'seq', 'head')), parts along dimension 0, may hold values from -6 to 6
- x_branch: bfloat16 [4096, 4096], P(('groups', 'seq'), 'head'), parts along dimension 0, may hold values from -6 to 6
- merge_list: int32 [4096, 2], P(('groups', 'seq')), parts along dimension 0, may hold values from 0 to 127
- lengths: int32 [32], P(('groups', 'seq')), parts along dimension 0, may hold values from 48 to 128, as said below
- log_decay: float32 [64, 4096], P('head', ('groups', 'seq')), parts along dimension 1, may hold values from -1.3 to 0
- init_state: float32 [128, 64, 128], P(('groups', 'head')), parts along dimension 0, may hold values from -12 to 12
- state_proj: bfloat16 [4096, 256], P(None, 'head'), may hold values from -0.005859375 to 0.005859375
- rate_proj: bfloat16 [4096, 64], P(None, 'head'), may hold values from -0.1875 to 0.1875
- step_bias: float32 [64], P('head'), may hold values from -2 to 1
- skip_gain: float32 [64], P('head'), may hold values from 0.1 to 1.9
- out_proj: bfloat16 [4096, 4096], P('head'), may hold values from -0.09375 to 0.09375
Outputs:
- out: bfloat16 [4096, 4096], P(('groups', 'seq', 'head')), parts along dimension 0
The draws below stay inside these ranges and needn't reach their ends.
There are 2 independent parts, one for each index of `groups`. The reference program is written for one: setup_inputs(seed, part) draws one part's arguments, and reference() takes and returns one part's arrays. A program takes and returns all parts, laid end to end along the dimension named above; an argument that names none is the same for every part. Nothing has to cross between parts.
Inputs may be any that keep to these rules, and one draw needn't show every extreme that they name: `merge_list`: each entry is a row position inside its own row's aligned block of 128 token rows. `lengths`: the number of used rows at the start of an aligned block of 128 token rows; the other rows of the block are padding.
All inputs are finite; a program needn't handle non-finite values.
Results may differ from the reference program's by a relative error of at most 0.014.
Values may be sent and summed in bfloat16 or wider, within the bound.
A program may use at most 128 MiB of HBM per device.

```python
import math
import jax
import jax.numpy as jnp
from jax import lax

D = 4096
SHARD_ATTN_UNITS = 64
HEAD_DIM = 64
STATE = 128
BLOCK = 256
MERGE = 128
TOK_DEV = 512
SPAN_ITEMS = 2048
N_HEAD = 4


def draw_lengths(key, part):
    key = jax.random.fold_in(key, 5)
    split_seed_keys = jax.random.split(key, 2)
    block_total = SPAN_ITEMS // MERGE
    least_rows = 3 * MERGE // 8
    lengths_drawn = jax.random.randint(split_seed_keys[0], (block_total,), least_rows, MERGE + 1)
    short_block = jax.random.randint(split_seed_keys[1], (), 1, block_total)
    block_ids = jnp.arange(block_total, dtype=jnp.int32)
    lengths_drawn = jnp.where(block_ids == 0, MERGE, lengths_drawn)
    lengths_drawn = jnp.where(block_ids == short_block, least_rows, lengths_drawn)
    return lengths_drawn.astype(jnp.int32)


def draw_log_decay(key, part):
    key = jax.random.fold_in(key, 7)
    split_seed_keys = jax.random.split(key, 7)
    fast_cut = 5
    is_fast = jax.random.randint(split_seed_keys[0], (SHARD_ATTN_UNITS, 1), 0, 10) < fast_cut
    fast_rate = jax.random.uniform(split_seed_keys[1], (SHARD_ATTN_UNITS, 1), jnp.float32, 1.0 / 50.0, 1.0 / 30.0)
    slow_rate = jnp.exp(jax.random.uniform(split_seed_keys[2], (SHARD_ATTN_UNITS, 1), jnp.float32, math.log(0.15), math.log(0.6))) / SPAN_ITEMS
    noise_spread = jax.random.uniform(split_seed_keys[3], (SHARD_ATTN_UNITS, SPAN_ITEMS), jnp.float32, 0.5, 1.5)
    shard_multiplier = jnp.repeat(jax.random.uniform(split_seed_keys[4], (SHARD_ATTN_UNITS, SPAN_ITEMS // TOK_DEV), jnp.float32, 0.4, 1.6), TOK_DEV, axis=1)
    spike_location = jax.random.randint(split_seed_keys[5], (SHARD_ATTN_UNITS, 2), 0, SPAN_ITEMS)
    spike_magnitude = jax.random.uniform(split_seed_keys[6], (SHARD_ATTN_UNITS, 2), jnp.float32, 0.22, 0.6)
    sequence_indices = jnp.arange(SPAN_ITEMS, dtype=jnp.int32)
    spike_occurrences = spike_magnitude[:, 0:1] * (sequence_indices[None, :] == spike_location[:, 0:1]).astype(jnp.float32)
    spike_occurrences = spike_occurrences + spike_magnitude[:, 1:2] * (sequence_indices[None, :] == spike_location[:, 1:2]).astype(jnp.float32)
    resting_intensity = jnp.where(is_fast, fast_rate, slow_rate)
    return (-(resting_intensity * noise_spread * shard_multiplier) - spike_occurrences).astype(jnp.float32)


def place_ends(drawn, own_key, smallest, top_value):
    longest = drawn.shape.index(max(drawn.shape))
    spots = []
    for shift in (0, 1):
        where = [jax.random.randint(jax.random.fold_in(own_key, axis), (), 0, length) for axis, length in enumerate(drawn.shape)]
        where[longest] = (where[longest] + shift) % drawn.shape[longest]
        spots.append(tuple(where))
    return drawn.at[spots[0]].set(smallest).at[spots[1]].set(top_value)


def steps_of(key, extent, shards, smallest, high):
    gain, own = 1.0, jax.random.fold_in(key, 6)
    for dim, blocks in shards:
        heights = jnp.exp(jax.random.uniform(jax.random.fold_in(own, dim), (blocks,), jnp.float32, smallest / len(shards), high / len(shards)))
        gain = gain * jnp.repeat(heights, extent[dim] // blocks).reshape([-1 if axis == dim else 1 for axis in range(len(extent))])
    return gain


def scatter_about(own_key, dims, width, bound, cuts=(), kind=jnp.bfloat16):
    result = jax.random.normal(own_key, dims, jnp.float32) * width
    if len(cuts) > 0:
        result = steps_of(own_key, dims, cuts, -0.22, 0.18) * result
    return jnp.clip(result, min=-bound, max=bound).astype(kind)


def setup_inputs(seed: int = 0, part: int = 0) -> dict:
    key_list = jax.random.split(jax.random.key(seed), 12)
    own_keys = jax.random.split(jax.random.fold_in(key_list[11], part), 12)
    raw_tokens = scatter_about(own_keys[0], (SPAN_ITEMS, D), 1.0, 6.0, ((0, 16),))
    x_branch = scatter_about(own_keys[1], (SPAN_ITEMS, SHARD_ATTN_UNITS * HEAD_DIM), 1.0, 6.0, ((0, 4), (1, 4)))
    merge_list = place_ends(jax.random.randint(own_keys[2], (SPAN_ITEMS, 2), 0, MERGE), jax.random.fold_in(own_keys[2], 1), 0, MERGE - 1).astype(jnp.int32)
    lengths = draw_lengths(jax.random.fold_in(jax.random.fold_in(key_list[11], part), 71), part)
    log_decay = draw_log_decay(jax.random.fold_in(jax.random.fold_in(key_list[11], part), 71), part)
    init_state = scatter_about(own_keys[5], (SHARD_ATTN_UNITS, HEAD_DIM, STATE), 2.0, 12.0, ((0, 4),), jnp.float32)
    state_proj = scatter_about(key_list[6], (D, 2 * STATE), (300 * D) ** -0.5, 0.005859375, ((1, 4),))
    rate_proj = scatter_about(key_list[7], (D, SHARD_ATTN_UNITS), (D // 4) ** -0.5, 0.1875, ((1, 4),))
    step_bias = jnp.clip(-2.0 + 3.0 * jax.random.uniform(key_list[8], (SHARD_ATTN_UNITS,), jnp.float32) ** steps_of(key_list[8], (SHARD_ATTN_UNITS,), ((0, 4),), -0.2, 0.2), -2.0, 1.0)
    skip_gain = jnp.clip(1.0 + 0.18 * jax.random.normal(key_list[9], (SHARD_ATTN_UNITS,), jnp.float32), 0.1, 1.9)
    out_proj = scatter_about(key_list[10], (SHARD_ATTN_UNITS * HEAD_DIM, D), (SHARD_ATTN_UNITS * HEAD_DIM) ** -0.5, 0.09375, ((0, 4),))
    return {"raw_tokens": raw_tokens, "x_branch": x_branch, "merge_list": merge_list, "lengths": lengths, "log_decay": log_decay, "init_state": init_state, "state_proj": state_proj, "rate_proj": rate_proj, "step_bias": step_bias, "skip_gain": skip_gain, "out_proj": out_proj}


def merge_rows(row_block, merge_list):
    row_count = row_block.shape[0]
    block_start = (jnp.arange(row_count, dtype=jnp.int32) // MERGE) * MERGE
    first_rows = jnp.take(row_block, block_start + merge_list[:, 0].astype(jnp.int32), axis=0).astype(jnp.float32)
    second = jnp.take(row_block, block_start + merge_list[:, 1].astype(jnp.int32), axis=0).astype(jnp.float32)
    return ((first_rows + second) * 0.5).astype(jnp.bfloat16)


def reference(raw_tokens, x_branch, merge_list, lengths, log_decay, init_state, state_proj, rate_proj, step_bias, skip_gain, out_proj):
    slot_ids = jnp.arange(MERGE, dtype=jnp.int32)
    used_mask = (slot_ids[None, :] < lengths[:, None].astype(jnp.int32)).reshape(SPAN_ITEMS).astype(jnp.float32)
    merged = merge_rows(raw_tokens, merge_list)
    merged_x = merge_rows(x_branch, merge_list)
    state_maps = jnp.dot(merged, state_proj, preferred_element_type=jnp.float32).astype(jnp.bfloat16)
    rate_pre = jnp.dot(merged, rate_proj, preferred_element_type=jnp.float32)
    step_size = jax.nn.softplus(rate_pre + step_bias[None, :]) * used_mask[:, None]
    log_rate = log_decay * used_mask[None, :]
    block_count = SPAN_ITEMS // BLOCK
    x_blocks = merged_x.reshape(block_count, BLOCK, SHARD_ATTN_UNITS, HEAD_DIM)
    b_blocks = state_maps[:, :STATE].reshape(block_count, BLOCK, STATE)
    c_blocks = state_maps[:, STATE:].reshape(block_count, BLOCK, STATE)
    step_blocks = step_size.reshape(block_count, BLOCK, SHARD_ATTN_UNITS).transpose(0, 2, 1)
    rate_blocks = log_rate.reshape(SHARD_ATTN_UNITS, block_count, BLOCK).transpose(1, 0, 2)
    position = jnp.arange(BLOCK, dtype=jnp.int32)
    causal = position[:, None] >= position[None, :]

    def advance(carry_state, slices):
        x_slice, b_slice, c_slice, step_slice, rate_slice = slices
        cumulative = jnp.cumsum(rate_slice, axis=1)
        scores = jnp.dot(c_slice, b_slice.T, preferred_element_type=jnp.float32)
        spread = jnp.where(causal[None], cumulative[:, :, None] - cumulative[:, None, :], 0.0)
        decays = jnp.where(causal[None], jnp.exp(spread), 0.0)
        weight = (scores[None] * decays * step_slice[:, None, :]).astype(jnp.bfloat16)
        inside = jnp.einsum("hij,jhp->ihp", weight.astype(jnp.float32), x_slice.astype(jnp.float32))
        carried = carry_state.astype(jnp.bfloat16)
        across = jnp.einsum("in,hpn->ihp", c_slice.astype(jnp.float32), carried.astype(jnp.float32)) * jnp.exp(cumulative).T[:, :, None]
        scaled = (jnp.exp(cumulative[:, -1:] - cumulative) * step_slice).T[:, :, None] * x_slice.astype(jnp.float32)
        scaled = scaled.astype(jnp.bfloat16)
        fresh_state = jnp.einsum("jhp,jn->hpn", scaled.astype(jnp.float32), b_slice.astype(jnp.float32))
        next_state = jnp.exp(cumulative[:, -1])[:, None, None] * carry_state + fresh_state
        output = inside + across + skip_gain[None, :, None] * x_slice.astype(jnp.float32)
        return next_state, output

    end_state, outputs = lax.scan(advance, init_state, (x_blocks, b_blocks, c_blocks, step_blocks, rate_blocks))
    mixed = (outputs.reshape(SPAN_ITEMS, SHARD_ATTN_UNITS * HEAD_DIM) * used_mask[:, None]).astype(jnp.bfloat16)
    group_width = (SHARD_ATTN_UNITS // N_HEAD) * HEAD_DIM
    summed = jnp.zeros((SPAN_ITEMS, D), jnp.float32)
    for group_index in range(N_HEAD):
        low_col = group_index * group_width
        part_sum = jnp.dot(mixed[:, low_col:low_col + group_width], out_proj[low_col:low_col + group_width], preferred_element_type=jnp.float32).astype(jnp.bfloat16)
        part_sum = lax.optimization_barrier(part_sum)
        summed = summed + part_sum.astype(jnp.float32)
    return summed.astype(jnp.bfloat16)
```

```python
import functools

import jax
import jax.numpy as jnp
from jax import lax
from jax.experimental import pallas as pl
from jax.experimental.pallas import tpu as pltpu
from jax.sharding import PartitionSpec as P

STATE = 128
BLOCK = 256
MERGE = 128
LANES = 128
WEIGHT_PIECES = 4
STATE_PIECES = 4
OUT_PIECES = 8
MESH = pl.DeviceIdType.MESH
F32 = jnp.float32
BF16 = jnp.bfloat16
HIGH = lax.Precision.HIGHEST


def dot(a, b, precision=None):
    return jnp.dot(a, b, preferred_element_type=F32, precision=precision)


def dot_t(a, b, precision=None):
    return lax.dot_general(
        a, b, (((1,), (1,)), ((), ())), preferred_element_type=F32, precision=precision
    )


def kernel(
    seq_count,
    lengths,
    step_bias,
    skip_gain,
    merge_list,
    log_decay,
    init_state,
    raw_hbm,
    x_hbm,
    state_hbm,
    rate_hbm,
    proj_hbm,
    out_ref,
    raw,
    x_rows,
    proj,
    state_w,
    rate_w,
    pick,
    merged,
    merged_x,
    decay,
    enter_exp,
    last_factor,
    steps,
    maps,
    rate_send,
    rate_got,
    fresh,
    state_in,
    state_out,
    carried,
    inside,
    mixed,
    mine,
    pair_send,
    pair_got,
    cross_send,
    cross_got,
    load_sem,
    w_send,
    w_recv,
    m_send,
    m_recv,
    s_send,
    s_recv,
    p_send,
    p_recv,
    c_send,
    c_recv,
):
    head = lax.axis_index("head")
    rank = lax.axis_index("seq")
    core = lax.rem(head, 2)
    sib = head + 1 - 2 * core
    cross = lax.rem(head + 2, 4)
    diag = 3 - head
    heads = log_decay.shape[0]
    width = merged_x.shape[2]
    pairs = heads // 2
    model = raw.shape[1]
    piece = model // WEIGHT_PIECES

    loads = [
        pltpu.make_async_copy(raw_hbm, raw, load_sem.at[0]),
        pltpu.make_async_copy(x_hbm, x_rows, load_sem.at[1]),
        pltpu.make_async_copy(state_hbm, state_w.at[head], load_sem.at[2]),
        pltpu.make_async_copy(rate_hbm, rate_w.at[head], load_sem.at[3]),
        pltpu.make_async_copy(proj_hbm, proj, load_sem.at[4]),
    ]
    for load in loads:
        load.start()

    barrier = pltpu.get_barrier_semaphore()
    for peer in (sib, cross, diag):
        pl.semaphore_signal(barrier, inc=1, device_id={"head": peer}, device_id_type=MESH)
    for peer in (lax.rem(rank + 1, seq_count), lax.rem(rank + seq_count - 1, seq_count)):
        pl.semaphore_signal(barrier, inc=1, device_id={"seq": peer}, device_id_type=MESH)
    pl.semaphore_wait(barrier, 5)

    def weight_copies(kind, p, peer, owner, forward):
        span = pl.ds(p * piece, piece)
        out = []
        for which, (source, held) in enumerate(((state_hbm, state_w), (rate_hbm, rate_w))):
            out.append(
                pltpu.make_async_remote_copy(
                    src_ref=held.at[owner, :, span] if forward else source.at[:, span],
                    dst_ref=held.at[owner, :, span],
                    send_sem=w_send.at[kind, p, which],
                    recv_sem=w_recv.at[kind, p, which],
                    device_id={"head": peer},
                    device_id_type=MESH,
                )
            )
        return out

    to_cross = [weight_copies(0, p, cross, head, False) for p in range(WEIGHT_PIECES)]
    to_sib = [weight_copies(1, p, sib, head, False) for p in range(WEIGHT_PIECES)]
    passed = [weight_copies(2, p, sib, cross, True) for p in range(WEIGHT_PIECES)]
    for group in (to_cross, to_sib):
        for copies in group:
            for copy in copies:
                copy.start()

    row_id = lax.broadcasted_iota(jnp.int32, (MERGE, MERGE), 0)
    for b in range(4):
        chosen = merge_list[:, b * MERGE : (b + 1) * MERGE]
        first = jnp.where(row_id == chosen[0:1], 0.5, 0.0)
        second = jnp.where(row_id == chosen[1:2], 0.5, 0.0)
        pick[b] = jnp.transpose(first + second).astype(BF16)
    loads[0].wait()
    own_pick = pick[head]
    for p in range(WEIGHT_PIECES):
        cols = slice(p * piece, (p + 1) * piece)
        merged[:, cols] = dot(own_pick, raw[:, cols]).astype(BF16)
    loads[1].wait()
    for b in range(4):
        rows = slice(b * MERGE, (b + 1) * MERGE)
        to = slice((b % 2) * MERGE, (b % 2 + 1) * MERGE)
        merged_x[b // 2, to, :] = dot(pick[b], x_rows[rows, :]).astype(BF16)

    first_half = lax.broadcasted_iota(jnp.int32, (BLOCK, LANES), 1) < LANES // 2
    top_half = lax.broadcasted_iota(jnp.int32, (STATE, LANES), 1) < LANES // 2
    row_i = lax.broadcasted_iota(jnp.int32, (BLOCK, BLOCK), 0)
    col_i = lax.broadcasted_iota(jnp.int32, (BLOCK, BLOCK), 1)
    causal = row_i >= col_i
    lower = jnp.where(causal, 1.0, 0.0)
    upper = jnp.where(row_i <= col_i, 1.0, 0.0)
    lane_i = lax.broadcasted_iota(jnp.int32, (heads, BLOCK), 1)

    def used_lanes(k):
        limit = jnp.where(lane_i < MERGE, lengths[2 * k], lengths[2 * k + 1] + MERGE)
        return jnp.where(lane_i < limit, 1.0, 0.0)

    def pass_on(p):
        for copy in to_cross[p]:
            copy.wait_recv()
        for copy in passed[p]:
            copy.start()

    done = 0
    for k in range(2):
        rates = log_decay[:, k * BLOCK : (k + 1) * BLOCK] * used_lanes(k)
        along = dot(rates, upper, HIGH)
        down = dot_t(lower, rates, HIGH)
        last_factor[k] = jnp.exp(along[:, BLOCK - 1 : BLOCK] - along)
        grown = jnp.exp(down)
        for i in range(pairs):
            enter_exp[k, :, i * LANES : (i + 1) * LANES] = jnp.where(
                first_half, grown[:, 2 * i : 2 * i + 1], grown[:, 2 * i + 1 : 2 * i + 2]
            )
        for h in range(heads):
            spread = down[:, h : h + 1] - along[h : h + 1, :]
            decay[k, h] = jnp.exp(jnp.minimum(spread, 0.0)).astype(BF16)
            done += 1
            if done % (2 * heads // WEIGHT_PIECES) == 0:
                pass_on(done // (2 * heads // WEIGHT_PIECES) - 1)

    loads[2].wait()
    loads[3].wait()
    map_sum, rate_sum = None, None
    for p in range(WEIGHT_PIECES):
        for copy in to_sib[p] + passed[p]:
            copy.wait_recv()
        cols = slice(p * piece, (p + 1) * piece)
        tokens = merged[:, cols]
        map_part = dot_t(tokens, state_w[:, :, cols].reshape(2 * STATE, piece))
        rate_part = dot_t(rate_w[:, :, cols].reshape(4 * heads, piece), tokens)
        map_sum = map_part if p == 0 else map_sum + map_part
        rate_sum = rate_part if p == 0 else rate_sum + rate_part
    maps[head] = map_sum.astype(BF16)
    rate_send[...] = rate_sum.reshape(4, heads, MERGE)
    shared = []
    for which, peer in enumerate((cross, diag, sib)):
        for kind, (source, to) in enumerate(
            ((rate_send.at[peer], rate_got.at[head]), (maps.at[head], maps.at[head]))
        ):
            copy = pltpu.make_async_remote_copy(
                src_ref=source,
                dst_ref=to,
                send_sem=m_send.at[which, kind],
                recv_sem=m_recv.at[which, kind],
                device_id={"head": peer},
                device_id_type=MESH,
            )
            copy.start()
            shared.append(copy)
    rate_got[head] = rate_send[head]
    for copy in shared:
        copy.wait_recv()

    head_i = lax.broadcasted_iota(jnp.int32, (heads, BLOCK), 0)
    bias = jnp.zeros((heads, BLOCK), F32)
    for h in range(heads):
        bias = jnp.where(head_i == h, step_bias[h], bias)
    for k in range(2):
        value = jnp.concatenate([rate_got[2 * k], rate_got[2 * k + 1]], axis=1) + bias
        size = jnp.maximum(value, 0.0) + jnp.log1p(jnp.exp(-jnp.abs(value)))
        size = size * used_lanes(k)
        steps[k] = size
        factor = last_factor[k] * size
        b_part = maps[2 * k : 2 * k + 2, :, :STATE].reshape(BLOCK, STATE)
        b_turned = jnp.transpose(b_part.astype(F32))
        for i in range(pairs):
            cols = slice(i * LANES, (i + 1) * LANES)
            x_pair = merged_x[k, :, cols]
            one = dot((b_turned * factor[2 * i : 2 * i + 1]).astype(BF16), x_pair)
            two = dot((b_turned * factor[2 * i + 1 : 2 * i + 2]).astype(BF16), x_pair)
            fresh[k, :, cols] = jnp.where(top_half, one, two)

    state_width = width // STATE_PIECES
    onward = [
        pltpu.make_async_remote_copy(
            src_ref=state_out.at[q],
            dst_ref=state_in.at[q],
            send_sem=s_send.at[q],
            recv_sem=s_recv.at[q],
            device_id={"seq": lax.rem(rank + 1, seq_count)},
            device_id_type=MESH,
        )
        for q in range(STATE_PIECES)
    ]

    def advance(q):
        cols = slice(q * state_width, (q + 1) * state_width)
        entering = state_in[q]
        middle = (
            enter_exp[0, BLOCK - 1 : BLOCK, cols] * entering.astype(F32) + fresh[0, :, cols]
        )
        carried[0, :, cols] = entering
        carried[1, :, cols] = middle.astype(BF16)
        leaving = enter_exp[1, BLOCK - 1 : BLOCK, cols] * middle + fresh[1, :, cols]
        state_out[q] = leaving.astype(BF16)

        @pl.when(rank < seq_count - 1)
        def _():
            onward[q].start()

    def inside_of(k):
        both = maps[pl.ds(2 * k, 2)].reshape(BLOCK, 2 * STATE)
        scores = dot_t(both[:, STATE:], both[:, :STATE])
        scores = jnp.where(causal, scores, 0.0).astype(BF16)
        sizes = steps[k].astype(BF16)
        for i in range(pairs):
            cols = slice(i * LANES, (i + 1) * LANES)
            x_pair = merged_x[k, :, cols]
            one = dot(scores * (decay[k, 2 * i] * sizes[2 * i : 2 * i + 1]), x_pair)
            two = dot(scores * (decay[k, 2 * i + 1] * sizes[2 * i + 1 : 2 * i + 2]), x_pair)
            gains = jnp.where(first_half, skip_gain[2 * i], skip_gain[2 * i + 1])
            inside[:, cols] = jnp.where(first_half, one, two) + gains * x_pair.astype(F32)

    def mix(k):
        c_part = maps[pl.ds(2 * k, 2), :, STATE:].reshape(BLOCK, STATE)
        limit = jnp.where(row_i < MERGE, lengths[2 * k], lengths[2 * k + 1] + MERGE)
        used = row_i < limit
        for i in range(width // BLOCK):
            cols = slice(i * BLOCK, (i + 1) * BLOCK)
            across = dot(c_part, carried[k, :, cols]) * enter_exp[k, :, cols]
            value = jnp.where(used, inside[:, cols] + across, 0.0).astype(BF16)
            mixed[pl.ds(2 * k, 2), :, cols] = value.reshape(2, MERGE, BLOCK)

    far, near = cross // 2, head // 2

    @pl.when(rank == 0)
    def _():
        per = state_width // LANES
        for i in range(pairs):
            turned = jnp.transpose(init_state[2 * i : 2 * i + 2].reshape(LANES, STATE))
            at = slice((i % per) * LANES, (i % per + 1) * LANES)
            state_in[i // per, :, at] = turned.astype(BF16)
        for q in range(STATE_PIECES):
            advance(q)

    inside_of(far)

    @pl.when(rank > 0)
    def _():
        for q in range(STATE_PIECES):
            onward[q].wait_recv()
            advance(q)

    mix(far)

    out_width = model // OUT_PIECES
    loads[4].wait()

    def swap(turn, n):
        return pltpu.make_async_remote_copy(
            src_ref=pair_send.at[turn, n],
            dst_ref=pair_got.at[turn, n],
            send_sem=p_send.at[turn, n],
            recv_sem=p_recv.at[turn, n],
            device_id={"head": sib},
            device_id_type=MESH,
        )

    swaps = [[swap(turn, n) for n in range(OUT_PIECES)] for turn in range(2)]
    crossings = [
        pltpu.make_async_remote_copy(
            src_ref=cross_send.at[n],
            dst_ref=cross_got.at[n],
            send_sem=c_send.at[n],
            recv_sem=c_recv.at[n],
            device_id={"head": cross},
            device_id_type=MESH,
        )
        for n in range(OUT_PIECES)
    ]

    def send_across(n):
        swaps[0][n].wait_recv()
        cross_send[n] = (mine[n] + pair_got[0, n].astype(F32)).astype(BF16)
        crossings[n].start()

    rows = jnp.concatenate([mixed[diag], mixed[cross]], axis=0)
    for n in range(OUT_PIECES):
        cols = slice(n * out_width, (n + 1) * out_width)
        terms = dot(rows, proj[:, cols])
        pair_send[0, n] = terms[:MERGE].astype(BF16)
        swaps[0][n].start()
        mine[n] = terms[MERGE:]
        if n > 0:
            send_across(n - 1)
    send_across(OUT_PIECES - 1)

    inside_of(near)
    mix(near)
    rows = jnp.concatenate([mixed[sib], mixed[head]], axis=0)
    for n in range(OUT_PIECES):
        cols = slice(n * out_width, (n + 1) * out_width)
        terms = dot(rows, proj[:, cols])
        pair_send[1, n] = terms[:MERGE].astype(BF16)
        swaps[1][n].start()
        mine[n] = terms[MERGE:]
    for n in range(OUT_PIECES):
        cols = slice(n * out_width, (n + 1) * out_width)
        swaps[1][n].wait_recv()
        total = mine[n] + pair_got[1, n].astype(F32)
        crossings[n].wait_recv()
        out_ref[:, cols] = (total + cross_got[n].astype(F32)).astype(BF16)

    for group in to_cross + to_sib + passed:
        for copy in group:
            copy.wait_send()
    for copy in shared + swaps[0] + swaps[1] + crossings:
        copy.wait_send()

    @pl.when(rank < seq_count - 1)
    def _():
        for copy in onward:
            copy.wait_send()


def on_device(
    seq_count,
    raw_tokens,
    x_branch,
    merge_list,
    lengths,
    log_decay,
    init_state,
    state_proj,
    rate_proj,
    step_bias,
    skip_gain,
    out_proj,
):
    own_rows, model = raw_tokens.shape
    width = x_branch.shape[1]
    heads = log_decay.shape[0]
    out_width = model // OUT_PIECES
    blocks = x_branch.shape[0] // BLOCK
    state_width = width // STATE_PIECES
    smem = pl.BlockSpec(memory_space=pltpu.SMEM)
    vmem = pl.BlockSpec(memory_space=pltpu.VMEM)
    hbm = pl.BlockSpec(memory_space=pl.ANY)
    dma = pltpu.SemaphoreType.DMA
    return pl.pallas_call(
        functools.partial(kernel, seq_count),
        out_shape=jax.ShapeDtypeStruct((own_rows, model), BF16),
        in_specs=[smem] * 3 + [vmem] * 3 + [hbm] * 5,
        out_specs=vmem,
        scratch_shapes=[
            pltpu.VMEM(raw_tokens.shape, BF16),
            pltpu.VMEM(x_branch.shape, BF16),
            pltpu.VMEM(out_proj.shape, BF16),
            pltpu.VMEM((4, state_proj.shape[1], model), BF16),
            pltpu.VMEM((4, heads, model), BF16),
            pltpu.VMEM((4, MERGE, MERGE), BF16),
            pltpu.VMEM((own_rows, model), BF16),
            pltpu.VMEM((blocks, BLOCK, width), BF16),
            pltpu.VMEM((blocks, heads, BLOCK, BLOCK), BF16),
            pltpu.VMEM((blocks, BLOCK, width), F32),
            pltpu.VMEM((blocks, heads, BLOCK), F32),
            pltpu.VMEM((blocks, heads, BLOCK), F32),
            pltpu.VMEM((4, MERGE, 2 * STATE), BF16),
            pltpu.VMEM((4, heads, MERGE), F32),
            pltpu.VMEM((4, heads, MERGE), F32),
            pltpu.VMEM((blocks, STATE, width), F32),
            pltpu.VMEM((STATE_PIECES, STATE, state_width), BF16),
            pltpu.VMEM((STATE_PIECES, STATE, state_width), BF16),
            pltpu.VMEM((blocks, STATE, width), BF16),
            pltpu.VMEM((BLOCK, width), F32),
            pltpu.VMEM((4, MERGE, width), BF16),
            pltpu.VMEM((OUT_PIECES, MERGE, out_width), F32),
            pltpu.VMEM((2, OUT_PIECES, MERGE, out_width), BF16),
            pltpu.VMEM((2, OUT_PIECES, MERGE, out_width), BF16),
            pltpu.VMEM((OUT_PIECES, MERGE, out_width), BF16),
            pltpu.VMEM((OUT_PIECES, MERGE, out_width), BF16),
            dma((5,)),
            dma((3, WEIGHT_PIECES, 2)),
            dma((3, WEIGHT_PIECES, 2)),
            dma((3, 2)),
            dma((3, 2)),
            dma((STATE_PIECES,)),
            dma((STATE_PIECES,)),
            dma((2, OUT_PIECES)),
            dma((2, OUT_PIECES)),
            dma((OUT_PIECES,)),
            dma((OUT_PIECES,)),
        ],
        compiler_params=pltpu.CompilerParams(
            collective_id=0, has_side_effects=True, vmem_limit_bytes=56 * 1024 * 1024
        ),
    )(
        lengths,
        step_bias,
        skip_gain,
        merge_list.T,
        log_decay,
        init_state,
        raw_tokens,
        x_branch,
        state_proj.T,
        rate_proj.T,
        out_proj,
    )


def solution(mesh):
    return jax.shard_map(
        functools.partial(on_device, mesh.shape["seq"]),
        mesh=mesh,
        in_specs=(
            P(("groups", "seq", "head"), None),
            P(("groups", "seq"), "head"),
            P(("groups", "seq"), None),
            P(("groups", "seq")),
            P("head", ("groups", "seq")),
            P(("groups", "head"), None, None),
            P(None, "head"),
            P(None, "head"),
            P("head"),
            P("head"),
            P("head", None),
        ),
        out_specs=P(("groups", "seq", "head"), None),
        check_vma=False,
    )
```

```python
import functools

import jax
import jax.numpy as jnp
from jax import lax
from jax.experimental import pallas as pl
from jax.experimental.pallas import tpu as pltpu
from jax.sharding import PartitionSpec as P

STATE = 128
BLOCK = 256
MERGE = 128
LANES = 128
WEIGHT_PIECES = 4
STATE_PIECES = 8
OUT_PIECES = 8
MESH = pl.DeviceIdType.MESH
F32 = jnp.float32
BF16 = jnp.bfloat16
HIGH = lax.Precision.HIGHEST


def dot(a, b, precision=None):
    return jnp.dot(a, b, preferred_element_type=F32, precision=precision)


def dot_t(a, b, precision=None):
    return lax.dot_general(
        a, b, (((1,), (1,)), ((), ())), preferred_element_type=F32, precision=precision
    )


def kernel(
    seq_count,
    lengths,
    step_bias,
    skip_gain,
    merge_list,
    log_decay,
    init_state,
    raw_hbm,
    x_hbm,
    state_hbm,
    rate_hbm,
    proj_hbm,
    total_hbm,
    cross_got,
    raw,
    x_rows,
    proj,
    state_w,
    rate_w,
    pick,
    merged,
    merged_x,
    decay,
    enter_exp,
    last_factor,
    steps,
    b_maps,
    c_maps,
    rate_send,
    rate_got,
    fresh,
    state_in,
    state_out,
    carried,
    inside,
    mixed,
    mine,
    pair_send,
    pair_got,
    cross_send,
    total,
    load_sem,
    w_send,
    w_recv,
    m_send,
    m_recv,
    s_send,
    s_recv,
    p_send,
    p_recv,
    c_send,
    c_recv,
):
    head = lax.axis_index("head")
    rank = lax.axis_index("seq")
    group = lax.axis_index("groups")
    core = lax.rem(head, 2)
    sib = head + 1 - 2 * core
    cross = lax.rem(head + 2, 4)
    diag = 3 - head
    heads = log_decay.shape[0]
    width = merged_x.shape[2]
    pairs = heads // 2
    model = raw.shape[1]
    piece = model // (2 * WEIGHT_PIECES)

    loads = [
        pltpu.make_async_copy(raw_hbm, raw, load_sem.at[0]),
        pltpu.make_async_copy(x_hbm, x_rows, load_sem.at[1]),
        pltpu.make_async_copy(state_hbm, state_w.at[head], load_sem.at[2]),
        pltpu.make_async_copy(rate_hbm, rate_w.at[head], load_sem.at[3]),
        pltpu.make_async_copy(proj_hbm, proj, load_sem.at[4]),
    ]
    for load in loads:
        load.start()

    barrier = pltpu.get_barrier_semaphore()
    for peer in (sib, cross, diag):
        pl.semaphore_signal(barrier, inc=1, device_id={"head": peer}, device_id_type=MESH)
    for peer in (lax.rem(rank + 1, seq_count), lax.rem(rank + seq_count - 1, seq_count)):
        pl.semaphore_signal(barrier, inc=1, device_id={"seq": peer}, device_id_type=MESH)
    pl.semaphore_signal(barrier, inc=1, device_id={"groups": 1 - group}, device_id_type=MESH)
    pl.semaphore_wait(barrier, 6)

    def piece_at(half, p):
        return pl.ds(pl.multiple_of((half * WEIGHT_PIECES + p) * piece, piece), piece)

    def weight_copies(kind, p, peer, owner, span, forward):
        out = []
        for which, (source, held) in enumerate(((state_hbm, state_w), (rate_hbm, rate_w))):
            out.append(
                pltpu.make_async_remote_copy(
                    src_ref=held.at[owner, :, span] if forward else source.at[:, span],
                    dst_ref=held.at[owner, :, span],
                    send_sem=w_send.at[kind, p, which],
                    recv_sem=w_recv.at[kind, p, which],
                    device_id=peer,
                    device_id_type=MESH,
                )
            )
        return out

    order = range(WEIGHT_PIECES)
    other = {"groups": 1 - group}
    near_by = {"head": sib}
    to_cross = [
        weight_copies(0, p, {"head": cross}, head, piece_at(group, p), False) for p in order
    ]
    to_sib = weight_copies(1, 0, near_by, head, pl.ds(0, model), False)
    to_group = [weight_copies(2, p, other, cross, piece_at(group, p), True) for p in order]
    pass_first = [weight_copies(3, p, near_by, cross, piece_at(group, p), True) for p in order]
    pass_second = [
        weight_copies(4, p, near_by, cross, piece_at(1 - group, p), True) for p in order
    ]
    for copy in sum(to_cross, []) + to_sib:
        copy.start()

    row_id = lax.broadcasted_iota(jnp.int32, (MERGE, MERGE), 0)
    for b in range(4):
        chosen = merge_list[:, b * MERGE : (b + 1) * MERGE]
        first = jnp.where(row_id == chosen[0:1], 0.5, 0.0)
        second = jnp.where(row_id == chosen[1:2], 0.5, 0.0)
        pick[b] = jnp.transpose(first + second).astype(BF16)
    loads[0].wait()
    own_pick = pick[head]
    for p in range(2 * WEIGHT_PIECES):
        cols = slice(p * piece, (p + 1) * piece)
        merged[:, cols] = dot(own_pick, raw[:, cols]).astype(BF16)
    loads[1].wait()
    for b in range(4):
        rows = slice(b * MERGE, (b + 1) * MERGE)
        to = slice((b % 2) * MERGE, (b % 2 + 1) * MERGE)
        merged_x[b // 2, to, :] = dot(pick[b], x_rows[rows, :]).astype(BF16)

    first_half = lax.broadcasted_iota(jnp.int32, (BLOCK, LANES), 1) < LANES // 2
    top_half = lax.broadcasted_iota(jnp.int32, (STATE, LANES), 1) < LANES // 2
    row_i = lax.broadcasted_iota(jnp.int32, (BLOCK, BLOCK), 0)
    col_i = lax.broadcasted_iota(jnp.int32, (BLOCK, BLOCK), 1)
    causal = row_i >= col_i
    lower = jnp.where(causal, 1.0, 0.0)
    upper = jnp.where(row_i <= col_i, 1.0, 0.0)
    lane_i = lax.broadcasted_iota(jnp.int32, (heads, BLOCK), 1)

    def used_lanes(k):
        limit = jnp.where(lane_i < MERGE, lengths[2 * k], lengths[2 * k + 1] + MERGE)
        return jnp.where(lane_i < limit, 1.0, 0.0)

    def pass_x(p):
        for copy in to_cross[p]:
            copy.wait_recv()
        for copy in to_group[p] + pass_first[p]:
            copy.start()

    def pass_y(p):
        for copy in to_group[p]:
            copy.wait_recv()
        for copy in pass_second[p]:
            copy.start()

    passes = [functools.partial(pass_x, 0)]
    for p in range(1, WEIGHT_PIECES):
        passes += [functools.partial(pass_x, p), functools.partial(pass_y, p - 1)]
    passes.append(functools.partial(pass_y, WEIGHT_PIECES - 1))

    done = 0
    for k in range(2):
        rates = log_decay[:, k * BLOCK : (k + 1) * BLOCK] * used_lanes(k)
        along = dot(rates, upper, HIGH)
        down = dot_t(lower, rates, HIGH)
        last_factor[k] = jnp.exp(along[:, BLOCK - 1 : BLOCK] - along)
        grown = jnp.exp(down)
        for i in range(pairs):
            enter_exp[k, :, i * LANES : (i + 1) * LANES] = jnp.where(
                first_half, grown[:, 2 * i : 2 * i + 1], grown[:, 2 * i + 1 : 2 * i + 2]
            )
        for h in range(heads):
            spread = down[:, h : h + 1] - along[h : h + 1, :]
            decay[k, h] = jnp.exp(jnp.minimum(spread, 0.0)).astype(BF16)
            done += 1
            if done % (2 * heads // len(passes)) == 0:
                passes[done // (2 * heads // len(passes)) - 1]()

    loads[2].wait()
    loads[3].wait()
    map_sum, rate_sum = None, None
    for copy in to_sib:
        copy.wait_recv()
    for p in range(2 * WEIGHT_PIECES):
        part = p % WEIGHT_PIECES
        for copy in (pass_first if p < WEIGHT_PIECES else pass_second)[part]:
            copy.wait_recv()
        cols = piece_at(group if p < WEIGHT_PIECES else 1 - group, part)
        tokens = merged[:, cols]
        map_part = dot_t(tokens, state_w[:, :, cols].reshape(2 * STATE, piece))
        rate_part = dot_t(rate_w[:, :, cols].reshape(4 * heads, piece), tokens)
        map_sum = map_part if p == 0 else map_sum + map_part
        rate_sum = rate_part if p == 0 else rate_sum + rate_part
    b_maps[head] = map_sum[:, :STATE].astype(BF16)
    c_maps[head] = map_sum[:, STATE:].astype(BF16)
    rate_send[...] = rate_sum.reshape(4, heads, MERGE)
    shared = [[], [], []]
    for kind, to in enumerate((rate_got, b_maps, c_maps)):
        for which, peer in enumerate((cross, diag, sib)):
            copy = pltpu.make_async_remote_copy(
                src_ref=rate_send.at[peer] if kind == 0 else to.at[head],
                dst_ref=to.at[head],
                send_sem=m_send.at[which, kind],
                recv_sem=m_recv.at[which, kind],
                device_id={"head": peer},
                device_id_type=MESH,
            )
            copy.start()
            shared[kind].append(copy)
    rate_got[head] = rate_send[head]

    state_width = width // STATE_PIECES
    onward = [
        pltpu.make_async_remote_copy(
            src_ref=state_out.at[q],
            dst_ref=state_in.at[q],
            send_sem=s_send.at[q],
            recv_sem=s_recv.at[q],
            device_id={"seq": lax.rem(rank + 1, seq_count)},
            device_id_type=MESH,
        )
        for q in range(STATE_PIECES)
    ]

    def advance(q):
        cols = slice(q * state_width, (q + 1) * state_width)
        entering = state_in[q]
        middle = (
            enter_exp[0, BLOCK - 1 : BLOCK, cols] * entering.astype(F32) + fresh[0, :, cols]
        )
        carried[0, :, cols] = entering
        carried[1, :, cols] = middle.astype(BF16)
        leaving = enter_exp[1, BLOCK - 1 : BLOCK, cols] * middle + fresh[1, :, cols]
        state_out[q] = leaving.astype(BF16)

        @pl.when(rank < seq_count - 1)
        def _():
            onward[q].start()

    head_i = lax.broadcasted_iota(jnp.int32, (heads, BLOCK), 0)
    bias = jnp.zeros((heads, BLOCK), F32)
    for h in range(heads):
        bias = jnp.where(head_i == h, step_bias[h], bias)
    for copy in shared[0]:
        copy.wait_recv()
    factors = []
    for k in range(2):
        value = jnp.concatenate([rate_got[2 * k], rate_got[2 * k + 1]], axis=1) + bias
        size = jnp.maximum(value, 0.0) + jnp.log1p(jnp.exp(-jnp.abs(value)))
        size = size * used_lanes(k)
        steps[k] = size
        factors.append(last_factor[k] * size)
    for copy in shared[1]:
        copy.wait_recv()
    turned_maps = [
        jnp.transpose(b_maps[2 * k : 2 * k + 2].reshape(BLOCK, STATE).astype(F32))
        for k in range(2)
    ]
    for i in range(pairs):
        cols = slice(i * LANES, (i + 1) * LANES)
        for k in range(2):
            x_pair = merged_x[k, :, cols]
            one, two = [
                dot((turned_maps[k] * factors[k][h : h + 1]).astype(BF16), x_pair)
                for h in (2 * i, 2 * i + 1)
            ]
            fresh[k, :, cols] = jnp.where(top_half, one, two)

        @pl.when(rank == 0)
        def _():
            turned = jnp.transpose(init_state[2 * i : 2 * i + 2].reshape(LANES, STATE))
            state_in[i] = turned.astype(BF16)
            advance(i)

    def inside_of(k):
        b_part = b_maps[pl.ds(2 * k, 2)].reshape(BLOCK, STATE)
        c_part = c_maps[pl.ds(2 * k, 2)].reshape(BLOCK, STATE)
        scores = dot_t(c_part, b_part)
        scores = jnp.where(causal, scores, 0.0).astype(BF16)
        sizes = steps[k].astype(BF16)
        for i in range(pairs):
            cols = slice(i * LANES, (i + 1) * LANES)
            x_pair = merged_x[k, :, cols]
            one = dot(scores * (decay[k, 2 * i] * sizes[2 * i : 2 * i + 1]), x_pair)
            two = dot(scores * (decay[k, 2 * i + 1] * sizes[2 * i + 1 : 2 * i + 2]), x_pair)
            gains = jnp.where(first_half, skip_gain[2 * i], skip_gain[2 * i + 1])
            inside[:, cols] = jnp.where(first_half, one, two) + gains * x_pair.astype(F32)

    def mix(k):
        c_part = c_maps[pl.ds(2 * k, 2)].reshape(BLOCK, STATE)
        limit = jnp.where(row_i < MERGE, lengths[2 * k], lengths[2 * k + 1] + MERGE)
        used = row_i < limit
        for i in range(width // BLOCK):
            cols = slice(i * BLOCK, (i + 1) * BLOCK)
            across = dot(c_part, carried[k, :, cols]) * enter_exp[k, :, cols]
            value = jnp.where(used, inside[:, cols] + across, 0.0).astype(BF16)
            mixed[pl.ds(2 * k, 2), :, cols] = value.reshape(2, MERGE, BLOCK)

    far, near = cross // 2, head // 2

    @pl.when(rank == 1)
    def _():
        for q in range(STATE_PIECES):
            onward[q].wait_recv()
            advance(q)

    for copy in shared[2]:
        copy.wait_recv()
    inside_of(far)

    @pl.when(rank > 1)
    def _():
        for q in range(STATE_PIECES):
            onward[q].wait_recv()
            advance(q)

    mix(far)

    out_width = model // OUT_PIECES
    loads[4].wait()

    def swap(turn, n):
        return pltpu.make_async_remote_copy(
            src_ref=pair_send.at[turn, n],
            dst_ref=pair_got.at[turn, n],
            send_sem=p_send.at[turn, n],
            recv_sem=p_recv.at[turn, n],
            device_id={"head": sib},
            device_id_type=MESH,
        )

    swaps = [[swap(turn, n) for n in range(OUT_PIECES)] for turn in range(2)]
    crossings = [
        pltpu.make_async_remote_copy(
            src_ref=cross_send.at[n],
            dst_ref=cross_got.at[:, n * out_width : (n + 1) * out_width],
            send_sem=c_send.at[n],
            recv_sem=c_recv.at[n],
            device_id={"head": cross},
            device_id_type=MESH,
        )
        for n in range(OUT_PIECES)
    ]

    def send_across(n):
        swaps[0][n].wait_recv()
        cross_send[n] = (mine[n] + pair_got[0, n].astype(F32)).astype(BF16)
        crossings[n].start()

    rows = jnp.concatenate([mixed[diag], mixed[cross]], axis=0)
    for n in range(OUT_PIECES):
        cols = slice(n * out_width, (n + 1) * out_width)
        terms = dot(rows, proj[:, cols])
        pair_send[0, n] = terms[:MERGE].astype(BF16)
        swaps[0][n].start()
        mine[n] = terms[MERGE:]
        if n > 0:
            send_across(n - 1)
    send_across(OUT_PIECES - 1)

    inside_of(near)
    mix(near)
    rows = jnp.concatenate([mixed[sib], mixed[head]], axis=0)
    for n in range(OUT_PIECES):
        cols = slice(n * out_width, (n + 1) * out_width)
        terms = dot(rows, proj[:, cols])
        pair_send[1, n] = terms[:MERGE].astype(BF16)
        swaps[1][n].start()
        mine[n] = terms[MERGE:]
    for n in range(OUT_PIECES):
        cols = slice(n * out_width, (n + 1) * out_width)
        swaps[1][n].wait_recv()
        total[:, cols] = (mine[n] + pair_got[1, n].astype(F32)).astype(BF16)
    store = pltpu.make_async_copy(total, total_hbm, load_sem.at[5])
    store.start()

    groups = to_cross + [to_sib] + to_group + pass_first + pass_second + shared + swaps
    for copy in sum(groups, []):
        copy.wait_send()
    store.wait()
    for copy in crossings:
        copy.wait()

    @pl.when(rank < seq_count - 1)
    def _():
        for copy in onward:
            copy.wait_send()


def on_device(
    seq_count,
    raw_tokens,
    x_branch,
    merge_list,
    lengths,
    log_decay,
    init_state,
    state_proj,
    rate_proj,
    step_bias,
    skip_gain,
    out_proj,
):
    own_rows, model = raw_tokens.shape
    width = x_branch.shape[1]
    heads = log_decay.shape[0]
    out_width = model // OUT_PIECES
    blocks = x_branch.shape[0] // BLOCK
    state_width = width // STATE_PIECES
    smem = pl.BlockSpec(memory_space=pltpu.SMEM)
    vmem = pl.BlockSpec(memory_space=pltpu.VMEM)
    hbm = pl.BlockSpec(memory_space=pl.ANY)
    dma = pltpu.SemaphoreType.DMA
    total, arrived = pl.pallas_call(
        functools.partial(kernel, seq_count),
        out_shape=[jax.ShapeDtypeStruct((own_rows, model), BF16)] * 2,
        in_specs=[smem] * 3 + [vmem] * 3 + [hbm] * 5,
        out_specs=[hbm, hbm],
        scratch_shapes=[
            pltpu.VMEM(raw_tokens.shape, BF16),
            pltpu.VMEM(x_branch.shape, BF16),
            pltpu.VMEM(out_proj.shape, BF16),
            pltpu.VMEM((4, state_proj.shape[1], model), BF16),
            pltpu.VMEM((4, heads, model), BF16),
            pltpu.VMEM((4, MERGE, MERGE), BF16),
            pltpu.VMEM((own_rows, model), BF16),
            pltpu.VMEM((blocks, BLOCK, width), BF16),
            pltpu.VMEM((blocks, heads, BLOCK, BLOCK), BF16),
            pltpu.VMEM((blocks, BLOCK, width), F32),
            pltpu.VMEM((blocks, heads, BLOCK), F32),
            pltpu.VMEM((blocks, heads, BLOCK), F32),
            pltpu.VMEM((4, MERGE, STATE), BF16),
            pltpu.VMEM((4, MERGE, STATE), BF16),
            pltpu.VMEM((4, heads, MERGE), F32),
            pltpu.VMEM((4, heads, MERGE), F32),
            pltpu.VMEM((blocks, STATE, width), F32),
            pltpu.VMEM((STATE_PIECES, STATE, state_width), BF16),
            pltpu.VMEM((STATE_PIECES, STATE, state_width), BF16),
            pltpu.VMEM((blocks, STATE, width), BF16),
            pltpu.VMEM((BLOCK, width), F32),
            pltpu.VMEM((4, MERGE, width), BF16),
            pltpu.VMEM((OUT_PIECES, MERGE, out_width), F32),
            pltpu.VMEM((2, OUT_PIECES, MERGE, out_width), BF16),
            pltpu.VMEM((2, OUT_PIECES, MERGE, out_width), BF16),
            pltpu.VMEM((OUT_PIECES, MERGE, out_width), BF16),
            pltpu.VMEM((own_rows, model), BF16),
            dma((6,)),
            dma((5, WEIGHT_PIECES, 2)),
            dma((5, WEIGHT_PIECES, 2)),
            dma((3, 3)),
            dma((3, 3)),
            dma((STATE_PIECES,)),
            dma((STATE_PIECES,)),
            dma((2, OUT_PIECES)),
            dma((2, OUT_PIECES)),
            dma((OUT_PIECES,)),
            dma((OUT_PIECES,)),
        ],
        compiler_params=pltpu.CompilerParams(
            collective_id=0, has_side_effects=True, vmem_limit_bytes=56 * 1024 * 1024
        ),
    )(
        lengths,
        step_bias,
        skip_gain,
        merge_list.T,
        log_decay,
        init_state,
        raw_tokens,
        x_branch,
        state_proj.T,
        rate_proj.T,
        out_proj,
    )
    return (total.astype(F32) + arrived.astype(F32)).astype(BF16)


def solution(mesh):
    return jax.shard_map(
        functools.partial(on_device, mesh.shape["seq"]),
        mesh=mesh,
        in_specs=(
            P(("groups", "seq", "head"), None),
            P(("groups", "seq"), "head"),
            P(("groups", "seq"), None),
            P(("groups", "seq")),
            P("head", ("groups", "seq")),
            P(("groups", "head"), None, None),
            P(None, "head"),
            P(None, "head"),
            P("head"),
            P("head"),
            P("head", None),
        ),
        out_specs=P(("groups", "seq", "head"), None),
        check_vma=False,
    )
```

```python
import functools

import jax
import jax.numpy as jnp
from jax import lax
from jax.experimental import pallas as pl
from jax.experimental.pallas import tpu as pltpu
from jax.sharding import PartitionSpec as P

STATE = 128
BLOCK = 256
MERGE = 128
LANES = 128
WEIGHT_PIECES = 4
STATE_PIECES = 8
OUT_PIECES = 8
MESH = pl.DeviceIdType.MESH
F32 = jnp.float32
BF16 = jnp.bfloat16
HIGH = lax.Precision.HIGHEST


def dot(a, b, precision=None):
    return jnp.dot(a, b, preferred_element_type=F32, precision=precision)


def dot_t(a, b, precision=None):
    return lax.dot_general(
        a, b, (((1,), (1,)), ((), ())), preferred_element_type=F32, precision=precision
    )


def kernel(
    seq_count,
    lengths,
    step_bias,
    skip_gain,
    merge_list,
    log_decay,
    init_hbm,
    raw_hbm,
    x_hbm,
    state_hbm,
    rate_hbm,
    proj_hbm,
    total_hbm,
    cross_got,
    raw,
    x_rows,
    proj,
    state_w,
    rate_w,
    pick,
    merged,
    merged_x,
    decay,
    enter_exp,
    last_factor,
    steps,
    b_maps,
    c_maps,
    rate_send,
    rate_got,
    fresh,
    state_in,
    state_out,
    carried,
    inside,
    mixed,
    mine,
    pair_send,
    pair_got,
    cross_send,
    total,
    init_state,
    load_sem,
    w_send,
    w_recv,
    m_send,
    m_recv,
    s_send,
    s_recv,
    p_send,
    p_recv,
    c_send,
    c_recv,
):
    head = lax.axis_index("head")
    rank = lax.axis_index("seq")
    group = lax.axis_index("groups")
    core = lax.rem(head, 2)
    sib = head + 1 - 2 * core
    cross = lax.rem(head + 2, 4)
    diag = 3 - head
    heads = log_decay.shape[0]
    width = merged_x.shape[2]
    pairs = heads // 2
    model = raw.shape[1]
    piece = model // (2 * WEIGHT_PIECES)

    barrier = pltpu.get_barrier_semaphore()
    for peer in (sib, cross, diag):
        pl.semaphore_signal(barrier, inc=1, device_id={"head": peer}, device_id_type=MESH)
    for peer in (lax.rem(rank + 1, seq_count), lax.rem(rank + seq_count - 1, seq_count)):
        pl.semaphore_signal(barrier, inc=1, device_id={"seq": peer}, device_id_type=MESH)
    pl.semaphore_signal(barrier, inc=1, device_id={"groups": 1 - group}, device_id_type=MESH)
    loads = [
        pltpu.make_async_copy(raw_hbm, raw, load_sem.at[0]),
        pltpu.make_async_copy(x_hbm, x_rows, load_sem.at[1]),
        pltpu.make_async_copy(state_hbm, state_w.at[head], load_sem.at[2]),
        pltpu.make_async_copy(rate_hbm, rate_w.at[head], load_sem.at[3]),
        pltpu.make_async_copy(proj_hbm, proj, load_sem.at[4]),
        pltpu.make_async_copy(init_hbm, init_state, load_sem.at[6]),
    ]
    for load in loads[:4]:
        load.start()
    pl.semaphore_wait(barrier, 6)

    def piece_at(half, p):
        return pl.ds(pl.multiple_of((half * WEIGHT_PIECES + p) * piece, piece), piece)

    def weight_copies(kind, p, peer, owner, span, forward):
        out = []
        for which, (source, held) in enumerate(((state_hbm, state_w), (rate_hbm, rate_w))):
            out.append(
                pltpu.make_async_remote_copy(
                    src_ref=held.at[owner, :, span] if forward else source.at[:, span],
                    dst_ref=held.at[owner, :, span],
                    send_sem=w_send.at[kind, p, which],
                    recv_sem=w_recv.at[kind, p, which],
                    device_id=peer,
                    device_id_type=MESH,
                )
            )
        return out

    order = range(WEIGHT_PIECES)
    other = {"groups": 1 - group}
    near_by = {"head": sib}
    to_cross = [
        weight_copies(0, p, {"head": cross}, head, piece_at(group, p), False) for p in order
    ]
    to_sib = weight_copies(1, 0, near_by, head, pl.ds(0, model), False)
    to_group = [weight_copies(2, p, other, cross, piece_at(group, p), True) for p in order]
    pass_first = [weight_copies(3, p, near_by, cross, piece_at(group, p), True) for p in order]
    pass_second = [
        weight_copies(4, p, near_by, cross, piece_at(1 - group, p), True) for p in order
    ]
    for copy in sum(to_cross, []) + to_sib:
        copy.start()

    row_id = lax.broadcasted_iota(jnp.int32, (MERGE, MERGE), 0)
    for b in range(4):
        chosen = merge_list[:, b * MERGE : (b + 1) * MERGE]
        first = jnp.where(row_id == chosen[0:1], 0.5, 0.0)
        second = jnp.where(row_id == chosen[1:2], 0.5, 0.0)
        pick[b] = jnp.transpose(first + second).astype(BF16)
    loads[0].wait()
    own_pick = pick[head]
    for p in range(2 * WEIGHT_PIECES):
        cols = slice(p * piece, (p + 1) * piece)
        merged[:, cols] = dot(own_pick, raw[:, cols]).astype(BF16)
    loads[1].wait()
    for b in range(4):
        rows = slice(b * MERGE, (b + 1) * MERGE)
        to = slice((b % 2) * MERGE, (b % 2 + 1) * MERGE)
        merged_x[b // 2, to, :] = dot(pick[b], x_rows[rows, :]).astype(BF16)

    first_half = lax.broadcasted_iota(jnp.int32, (BLOCK, LANES), 1) < LANES // 2
    top_half = lax.broadcasted_iota(jnp.int32, (STATE, LANES), 1) < LANES // 2
    row_i = lax.broadcasted_iota(jnp.int32, (BLOCK, BLOCK), 0)
    col_i = lax.broadcasted_iota(jnp.int32, (BLOCK, BLOCK), 1)
    causal = row_i >= col_i
    lower = jnp.where(causal, 1.0, 0.0)
    upper = jnp.where(row_i <= col_i, 1.0, 0.0)
    lane_i = lax.broadcasted_iota(jnp.int32, (heads, BLOCK), 1)

    def used_lanes(k):
        limit = jnp.where(lane_i < MERGE, lengths[2 * k], lengths[2 * k + 1] + MERGE)
        return jnp.where(lane_i < limit, 1.0, 0.0)

    def pass_x(p):
        for copy in to_cross[p]:
            copy.wait_recv()
        for copy in to_group[p] + pass_first[p]:
            copy.start()

    def pass_y(p):
        for copy in to_group[p]:
            copy.wait_recv()
        for copy in pass_second[p]:
            copy.start()

    passes = [functools.partial(pass_x, 0)]
    for p in range(1, WEIGHT_PIECES):
        passes += [functools.partial(pass_x, p), functools.partial(pass_y, p - 1)]
    passes.append(functools.partial(pass_y, WEIGHT_PIECES - 1))

    done = 0
    for k in range(2):
        rates = log_decay[:, k * BLOCK : (k + 1) * BLOCK] * used_lanes(k)
        along = dot(rates, upper, HIGH)
        down = dot_t(lower, rates, HIGH)
        last_factor[k] = jnp.exp(along[:, BLOCK - 1 : BLOCK] - along)
        grown = jnp.exp(down)
        for i in range(pairs):
            enter_exp[k, :, i * LANES : (i + 1) * LANES] = jnp.where(
                first_half, grown[:, 2 * i : 2 * i + 1], grown[:, 2 * i + 1 : 2 * i + 2]
            )
        for h in range(heads):
            spread = down[:, h : h + 1] - along[h : h + 1, :]
            decay[k, h] = jnp.exp(jnp.minimum(spread, 0.0)).astype(BF16)
            done += 1
            if done % (2 * heads // len(passes)) == 0:
                passes[done // (2 * heads // len(passes)) - 1]()

    loads[4].start()
    loads[5].start()

    loads[2].wait()
    loads[3].wait()
    map_sum, rate_sum = None, None
    for copy in to_sib:
        copy.wait_recv()
    for p in range(2 * WEIGHT_PIECES):
        part = p % WEIGHT_PIECES
        for copy in (pass_first if p < WEIGHT_PIECES else pass_second)[part]:
            copy.wait_recv()
        cols = piece_at(group if p < WEIGHT_PIECES else 1 - group, part)
        tokens = merged[:, cols]
        map_part = dot_t(tokens, state_w[:, :, cols].reshape(2 * STATE, piece))
        rate_part = dot_t(rate_w[:, :, cols].reshape(4 * heads, piece), tokens)
        map_sum = map_part if p == 0 else map_sum + map_part
        rate_sum = rate_part if p == 0 else rate_sum + rate_part
    b_maps[head] = map_sum[:, :STATE].astype(BF16)
    c_maps[head] = map_sum[:, STATE:].astype(BF16)
    rate_send[...] = rate_sum.reshape(4, heads, MERGE)
    shared = [[], [], []]
    for kind, to in enumerate((rate_got, b_maps, c_maps)):
        for which, peer in enumerate((cross, diag, sib)):
            copy = pltpu.make_async_remote_copy(
                src_ref=rate_send.at[peer] if kind == 0 else to.at[head],
                dst_ref=to.at[head],
                send_sem=m_send.at[which, kind],
                recv_sem=m_recv.at[which, kind],
                device_id={"head": peer},
                device_id_type=MESH,
            )
            copy.start()
            shared[kind].append(copy)
    rate_got[head] = rate_send[head]

    state_width = width // STATE_PIECES
    onward = [
        pltpu.make_async_remote_copy(
            src_ref=state_out.at[q],
            dst_ref=state_in.at[q],
            send_sem=s_send.at[q],
            recv_sem=s_recv.at[q],
            device_id={"seq": lax.rem(rank + 1, seq_count)},
            device_id_type=MESH,
        )
        for q in range(STATE_PIECES)
    ]

    def advance(q):
        cols = slice(q * state_width, (q + 1) * state_width)
        entering = state_in[q]
        middle = (
            enter_exp[0, BLOCK - 1 : BLOCK, cols] * entering.astype(F32) + fresh[0, :, cols]
        )
        carried[0, :, cols] = entering
        carried[1, :, cols] = middle.astype(BF16)
        leaving = enter_exp[1, BLOCK - 1 : BLOCK, cols] * middle + fresh[1, :, cols]
        state_out[q] = leaving.astype(BF16)

        @pl.when(rank < seq_count - 1)
        def _():
            onward[q].start()

    loads[5].wait()

    head_i = lax.broadcasted_iota(jnp.int32, (heads, BLOCK), 0)
    bias = jnp.zeros((heads, BLOCK), F32)
    for h in range(heads):
        bias = jnp.where(head_i == h, step_bias[h], bias)
    for copy in shared[0]:
        copy.wait_recv()
    factors = []
    for k in range(2):
        value = jnp.concatenate([rate_got[2 * k], rate_got[2 * k + 1]], axis=1) + bias
        size = jnp.maximum(value, 0.0) + jnp.log1p(jnp.exp(-jnp.abs(value)))
        size = size * used_lanes(k)
        steps[k] = size
        factors.append(last_factor[k] * size)
    for copy in shared[1]:
        copy.wait_recv()
    turned_maps = [
        jnp.transpose(b_maps[2 * k : 2 * k + 2].reshape(BLOCK, STATE).astype(F32))
        for k in range(2)
    ]
    for i in range(pairs):
        cols = slice(i * LANES, (i + 1) * LANES)
        for k in range(2):
            x_pair = merged_x[k, :, cols]
            one, two = [
                dot((turned_maps[k] * factors[k][h : h + 1]).astype(BF16), x_pair)
                for h in (2 * i, 2 * i + 1)
            ]
            fresh[k, :, cols] = jnp.where(top_half, one, two)

        @pl.when(rank == 0)
        def _():
            turned = jnp.transpose(init_state[2 * i : 2 * i + 2].reshape(LANES, STATE))
            state_in[i] = turned.astype(BF16)
            advance(i)

    def inside_of(k):
        b_part = b_maps[pl.ds(2 * k, 2)].reshape(BLOCK, STATE)
        c_part = c_maps[pl.ds(2 * k, 2)].reshape(BLOCK, STATE)
        scores = dot_t(c_part, b_part)
        scores = jnp.where(causal, scores, 0.0).astype(BF16)
        sizes = steps[k].astype(BF16)
        for i in range(pairs):
            cols = slice(i * LANES, (i + 1) * LANES)
            x_pair = merged_x[k, :, cols]
            one = dot(scores * (decay[k, 2 * i] * sizes[2 * i : 2 * i + 1]), x_pair)
            two = dot(scores * (decay[k, 2 * i + 1] * sizes[2 * i + 1 : 2 * i + 2]), x_pair)
            gains = jnp.where(first_half, skip_gain[2 * i], skip_gain[2 * i + 1])
            inside[:, cols] = jnp.where(first_half, one, two) + gains * x_pair.astype(F32)

    def mix(k):
        c_part = c_maps[pl.ds(2 * k, 2)].reshape(BLOCK, STATE)
        limit = jnp.where(row_i < MERGE, lengths[2 * k], lengths[2 * k + 1] + MERGE)
        used = row_i < limit
        for i in range(width // BLOCK):
            cols = slice(i * BLOCK, (i + 1) * BLOCK)
            across = dot(c_part, carried[k, :, cols]) * enter_exp[k, :, cols]
            value = jnp.where(used, inside[:, cols] + across, 0.0).astype(BF16)
            mixed[pl.ds(2 * k, 2), :, cols] = value.reshape(2, MERGE, BLOCK)

    far, near = cross // 2, head // 2

    @pl.when(rank == 1)
    def _():
        for q in range(STATE_PIECES):
            onward[q].wait_recv()
            advance(q)

    for copy in shared[2]:
        copy.wait_recv()
    inside_of(far)

    @pl.when(rank > 1)
    def _():
        for q in range(STATE_PIECES):
            onward[q].wait_recv()
            advance(q)

    mix(far)

    out_width = model // OUT_PIECES
    loads[4].wait()

    def swap(turn, n):
        return pltpu.make_async_remote_copy(
            src_ref=pair_send.at[turn, n],
            dst_ref=pair_got.at[turn, n],
            send_sem=p_send.at[turn, n],
            recv_sem=p_recv.at[turn, n],
            device_id={"head": sib},
            device_id_type=MESH,
        )

    swaps = [[swap(turn, n) for n in range(OUT_PIECES)] for turn in range(2)]
    crossings = [
        pltpu.make_async_remote_copy(
            src_ref=cross_send.at[n],
            dst_ref=cross_got.at[:, n * out_width : (n + 1) * out_width],
            send_sem=c_send.at[n],
            recv_sem=c_recv.at[n],
            device_id={"head": cross},
            device_id_type=MESH,
        )
        for n in range(OUT_PIECES)
    ]

    def send_across(n):
        swaps[0][n].wait_recv()
        cross_send[n] = (mine[n] + pair_got[0, n].astype(F32)).astype(BF16)
        crossings[n].start()

    rows = jnp.concatenate([mixed[diag], mixed[cross]], axis=0)
    for n in range(OUT_PIECES):
        cols = slice(n * out_width, (n + 1) * out_width)
        terms = dot(rows, proj[:, cols])
        pair_send[0, n] = terms[:MERGE].astype(BF16)
        swaps[0][n].start()
        mine[n] = terms[MERGE:]
        if n > 0:
            send_across(n - 1)
    send_across(OUT_PIECES - 1)

    inside_of(near)
    mix(near)
    rows = jnp.concatenate([mixed[sib], mixed[head]], axis=0)
    for n in range(OUT_PIECES):
        cols = slice(n * out_width, (n + 1) * out_width)
        terms = dot(rows, proj[:, cols])
        pair_send[1, n] = terms[:MERGE].astype(BF16)
        swaps[1][n].start()
        mine[n] = terms[MERGE:]
    for n in range(OUT_PIECES):
        cols = slice(n * out_width, (n + 1) * out_width)
        swaps[1][n].wait_recv()
        total[:, cols] = (mine[n] + pair_got[1, n].astype(F32)).astype(BF16)
    store = pltpu.make_async_copy(total, total_hbm, load_sem.at[5])
    store.start()

    groups = to_cross + [to_sib] + to_group + pass_first + pass_second + shared + swaps
    for copy in sum(groups, []):
        copy.wait_send()
    store.wait()
    for copy in crossings:
        copy.wait()

    @pl.when(rank < seq_count - 1)
    def _():
        for copy in onward:
            copy.wait_send()


def on_device(
    seq_count,
    raw_tokens,
    x_branch,
    merge_list,
    lengths,
    log_decay,
    init_state,
    state_proj,
    rate_proj,
    step_bias,
    skip_gain,
    out_proj,
):
    own_rows, model = raw_tokens.shape
    width = x_branch.shape[1]
    heads = log_decay.shape[0]
    out_width = model // OUT_PIECES
    blocks = x_branch.shape[0] // BLOCK
    state_width = width // STATE_PIECES
    smem = pl.BlockSpec(memory_space=pltpu.SMEM)
    vmem = pl.BlockSpec(memory_space=pltpu.VMEM)
    hbm = pl.BlockSpec(memory_space=pl.ANY)
    dma = pltpu.SemaphoreType.DMA
    total, arrived = pl.pallas_call(
        functools.partial(kernel, seq_count),
        out_shape=[jax.ShapeDtypeStruct((own_rows, model), BF16)] * 2,
        in_specs=[smem] * 3 + [vmem] * 2 + [hbm] * 6,
        out_specs=[hbm, hbm],
        scratch_shapes=[
            pltpu.VMEM(raw_tokens.shape, BF16),
            pltpu.VMEM(x_branch.shape, BF16),
            pltpu.VMEM(out_proj.shape, BF16),
            pltpu.VMEM((4, state_proj.shape[1], model), BF16),
            pltpu.VMEM((4, heads, model), BF16),
            pltpu.VMEM((4, MERGE, MERGE), BF16),
            pltpu.VMEM((own_rows, model), BF16),
            pltpu.VMEM((blocks, BLOCK, width), BF16),
            pltpu.VMEM((blocks, heads, BLOCK, BLOCK), BF16),
            pltpu.VMEM((blocks, BLOCK, width), F32),
            pltpu.VMEM((blocks, heads, BLOCK), F32),
            pltpu.VMEM((blocks, heads, BLOCK), F32),
            pltpu.VMEM((4, MERGE, STATE), BF16),
            pltpu.VMEM((4, MERGE, STATE), BF16),
            pltpu.VMEM((4, heads, MERGE), F32),
            pltpu.VMEM((4, heads, MERGE), F32),
            pltpu.VMEM((blocks, STATE, width), F32),
            pltpu.VMEM((STATE_PIECES, STATE, state_width), BF16),
            pltpu.VMEM((STATE_PIECES, STATE, state_width), BF16),
            pltpu.VMEM((blocks, STATE, width), BF16),
            pltpu.VMEM((BLOCK, width), F32),
            pltpu.VMEM((4, MERGE, width), BF16),
            pltpu.VMEM((OUT_PIECES, MERGE, out_width), F32),
            pltpu.VMEM((2, OUT_PIECES, MERGE, out_width), BF16),
            pltpu.VMEM((2, OUT_PIECES, MERGE, out_width), BF16),
            pltpu.VMEM((OUT_PIECES, MERGE, out_width), BF16),
            pltpu.VMEM((own_rows, model), BF16),
            pltpu.VMEM(init_state.shape, F32),
            dma((7,)),
            dma((5, WEIGHT_PIECES, 2)),
            dma((5, WEIGHT_PIECES, 2)),
            dma((3, 3)),
            dma((3, 3)),
            dma((STATE_PIECES,)),
            dma((STATE_PIECES,)),
            dma((2, OUT_PIECES)),
            dma((2, OUT_PIECES)),
            dma((OUT_PIECES,)),
            dma((OUT_PIECES,)),
        ],
        compiler_params=pltpu.CompilerParams(
            collective_id=0, has_side_effects=True, vmem_limit_bytes=56 * 1024 * 1024
        ),
    )(
        lengths,
        step_bias,
        skip_gain,
        merge_list.T,
        log_decay,
        init_state,
        raw_tokens,
        x_branch,
        state_proj.T,
        rate_proj.T,
        out_proj,
    )
    return (total.astype(F32) + arrived.astype(F32)).astype(BF16)


def solution(mesh):
    return jax.shard_map(
        functools.partial(on_device, mesh.shape["seq"]),
        mesh=mesh,
        in_specs=(
            P(("groups", "seq", "head"), None),
            P(("groups", "seq"), "head"),
            P(("groups", "seq"), None),
            P(("groups", "seq")),
            P("head", ("groups", "seq")),
            P(("groups", "head"), None, None),
            P(None, "head"),
            P(None, "head"),
            P("head"),
            P("head"),
            P("head", None),
        ),
        out_specs=P(("groups", "seq", "head"), None),
        check_vma=False,
    )
```
